32 devices in a mesh: groups: 2 (over y), seq: 4 (over z), mp: 2 (over x), batch: 2 (over core).
Axes of the slice: x: 2, y: 2, z: 4, core: 2. Of those that a mesh axis runs over, the one named last changes fastest.
Arguments:
- hidden: bfloat16 [4, 1024, 2048], P(('groups', 'batch'), 'seq', 'mp'), parts along dimension 0, may hold values from -6 to 6
- segment_ids: int32 [4, 1024], P(('groups', 'batch'), 'seq'), parts along dimension 0, may hold values from 0 to 3, never falling along the last dimension, each value on 1 to 512 neighbouring positions
- norm_gain: float32 [2048], replicated, may hold values from 0.1 to 1.9
- w_gate: bfloat16 [2048, 2048], P('seq', 'mp'), may hold values from -0.125 to 0.125
- w_value: bfloat16 [2048, 2048], P('seq', 'mp'), may hold values from -0.125 to 0.125
- w_in_out: bfloat16 [2048, 256], P('seq', 'mp'), may hold values from -0.125 to 0.125
- w_step: bfloat16 [2048, 32], P('seq', 'mp'), may hold values from -0.125 to 0.125
- step_bias: float32 [32], P('mp'), may hold values from -3 to -1
- decay_rate: float32 [32], P('mp'), may hold values from 0 to 1, as said below
- skip_gain: float32 [32], P('mp'), may hold values from 0.5 to 1.5
- conv_value: bfloat16 [4, 2048], P(None, 'mp'), may hold values from -3 to 3
- conv_in_out: bfloat16 [4, 256], P(None, 'mp'), may hold values from -3 to 3
- w_out: bfloat16 [2048, 2048], P('mp', 'seq'), may hold values from -0.125 to 0.125
Outputs:
- mixed_out: bfloat16 [4, 1024, 2048], P(('groups', 'batch'), 'seq', 'mp'), parts along dimension 0
The draws below stay inside these ranges and needn't reach their ends.
There are 2 independent parts, one for each index of `groups`. The reference program is written for one: setup_inputs(seed, part) draws one part's arguments, and reference() takes and returns one part's arrays. A program takes and returns all parts, laid end to end along the dimension named above; an argument that names none is the same for every part. Nothing has to cross between parts.
Inputs may be any that keep to these rules, and one draw needn't show every extreme that they name: `decay_rate`: each head's rate is positive and at most 0.15.
All inputs are finite; a program needn't handle non-finite values.
Results may differ from the reference program's by a relative error of at most 0.0076.
Values may be sent and summed in bfloat16 or wider, within the bound.
A program may use at most 64 MiB of HBM per device.

```python
import math
import jax
import jax.numpy as jnp
import numpy as np
from jax import lax

D = 2048
H = 32
P_SIZE = 64
NS = 128
CONV = 4
SPAN = 256
GROUP_HEADS = 8
SEGS = 4
DI = 2048
LENGTH = 1024
WINDOWS = 2


def draw_decay_rate(key, part):
    key = jax.random.fold_in(key, 7)
    uniform_draw = jax.random.uniform(key, (H,), jnp.float32)
    lowest = 1.0 / LENGTH
    return (lowest * (0.15 / lowest) ** uniform_draw).astype(jnp.float32)


def block_levels(key, shape, split, smallest, largest):
    def one(position, shards_of):
        draws = jax.random.uniform(jax.random.fold_in(jax.random.fold_in(key, 6), position), (shards_of,), jnp.float32, smallest / len(split), largest / len(split))
        return jnp.repeat(jnp.exp(draws), shape[position] // shards_of).reshape((-1,) + (1,) * (len(shape) - position - 1))

    loudness = one(*split[0])
    for cut in split[1:]:
        loudness = loudness * one(*cut)
    return loudness


def split_up(count, total, most, slope):
    portions = [(1 << 20) // math.isqrt(standing ** slope) + 1 for standing in range(2, count + 1)]
    rest, counts = total - most - (count - 1), [1] * (count - 1)
    while rest > 0:
        candidates = [i for i in range(count - 1) if counts[i] < most]
        mass, remaining = sum([portions[i] for i in candidates]), rest
        for i in candidates:
            addition = min(most - counts[i], max(1, remaining * portions[i] // mass), rest)
            counts[i] = counts[i] + addition
            rest = rest - addition
    return np.array([most] + counts)


def uneven_parts(key, number_of, total, reach, skew):
    if number_of == 2:
        one = jax.random.randint(key, (), max(1, total - reach), min(reach, total - 1) + 1)
        return jnp.stack([one, total - one])
    lengths = jnp.asarray(split_up(number_of, total, reach, skew), jnp.int32)
    pairs = (number_of - 1) // 2
    donor, taker = lengths[1:1 + 2 * pairs:2], lengths[2:2 + 2 * pairs:2]
    room = jnp.minimum(donor - 1, reach - taker)
    passed = jax.random.randint(jax.random.fold_in(key, 1), (pairs,), 0, 1 << 20) % (room + 1)
    lengths = lengths.at[1:1 + 2 * pairs:2].set(donor - passed).at[2:2 + 2 * pairs:2].set(taker + passed)
    return lengths[jax.random.permutation(jax.random.fold_in(key, 2), number_of)]


def noise(stream_key, shape, deviation, reach, split=(), kind=jnp.bfloat16):
    loudness = block_levels(stream_key, shape, split, -0.22, 0.18) if split else 1.0
    array = jax.random.normal(stream_key, shape, jnp.float32) * deviation * loudness
    return jnp.minimum(jnp.maximum(array, -reach), reach).astype(kind)


def setup_inputs(seed: int = 0, part: int = 0) -> dict:
    streams_of = jax.random.split(jax.random.key(seed), 14)
    part_keys = jax.random.split(jax.random.fold_in(streams_of[13], part), 14)
    return {
        "hidden": noise(part_keys[0], (WINDOWS, LENGTH, D), 1.0, 6.0, ((0, 2), (1, 4), (2, 2))),
        "segment_ids": jax.vmap(lambda own: jnp.searchsorted(jnp.cumsum(uneven_parts(own, SEGS, LENGTH, LENGTH // 2, 2)), jnp.arange(LENGTH), side="right"))(jax.random.split(part_keys[1], WINDOWS)).reshape((WINDOWS, LENGTH)).astype(jnp.int32),
        "norm_gain": jnp.clip(1.0 + 0.18 * jax.random.normal(streams_of[2], (D,), jnp.float32), 0.1, 1.9),
        "w_gate": noise(streams_of[3], (D, DI), D ** -0.5, 0.125, ((0, 4), (1, 2))),
        "w_value": noise(streams_of[4], (D, DI), D ** -0.5, 0.125, ((0, 4), (1, 2))),
        "w_in_out": noise(streams_of[5], (D, 2 * NS), D ** -0.5, 0.125, ((0, 4), (1, 2))),
        "w_step": noise(streams_of[6], (D, H), D ** -0.5, 0.125, ((0, 4), (1, 2))),
        "step_bias": jnp.clip(-3.0 + 2.0 * jax.random.uniform(streams_of[7], (H,), jnp.float32) ** block_levels(streams_of[7], (H,), ((0, 2),), -0.2, 0.2), -3.0, -1.0),
        "decay_rate": draw_decay_rate(jax.random.fold_in(streams_of[13], 71), part),
        "skip_gain": jnp.clip(0.5 + 1.0 * jax.random.uniform(streams_of[9], (H,), jnp.float32) ** block_levels(streams_of[9], (H,), ((0, 2),), -0.2, 0.2), 0.5, 1.5),
        "conv_value": noise(streams_of[10], (CONV, DI), CONV ** -0.5, 3.0, ((1, 2),)),
        "conv_in_out": noise(streams_of[11], (CONV, 2 * NS), CONV ** -0.5, 3.0, ((1, 2),)),
        "w_out": noise(streams_of[12], (DI, D), DI ** -0.5, 0.125, ((0, 2), (1, 4))),
    }


def span_terms(values, input_maps, output_maps, log_decay, step_size, segment, segment_before):
    span_rows = values.shape[0]
    cumulative = jnp.cumsum(log_decay, axis=0)
    scores = jnp.dot(output_maps, input_maps.T, preferred_element_type=jnp.float32)
    row_index = lax.broadcasted_iota(jnp.int32, (span_rows, span_rows), 0)
    col_index = lax.broadcasted_iota(jnp.int32, (span_rows, span_rows), 1)
    allowed = (segment[:, None] == segment[None, :]) & (col_index <= row_index)
    cum_heads = cumulative.T
    spread = cum_heads[:, :, None] - cum_heads[:, None, :]
    weights = jnp.where(allowed[None], jnp.exp(jnp.where(allowed[None], spread, 0.0)), 0.0)
    mixing = (scores[None] * weights * step_size.T[:, None, :]).astype(jnp.bfloat16)
    intra_part = jnp.einsum('hij,jhp->ihp', mixing.astype(jnp.float32), values.astype(jnp.float32))
    final_cum = cumulative[-1]
    same_end = (segment == segment[-1]).astype(jnp.float32)
    to_end = jnp.exp(final_cum[None] - cumulative) * step_size * same_end[:, None]
    weighted = (values.astype(jnp.float32) * to_end[:, :, None]).astype(jnp.bfloat16)
    span_state = jnp.einsum('jhp,jn->hpn', weighted.astype(jnp.float32), input_maps.astype(jnp.float32))
    inflow = jnp.exp(cumulative) * (segment == segment_before).astype(jnp.float32)[:, None]
    passing = jnp.exp(final_cum) * (segment[-1] == segment_before).astype(jnp.float32)
    return (intra_part, span_state, inflow, passing)

def causal_conv(series, kernel):
    reach_rows = kernel.shape[0] - 1
    length_rows = series.shape[0]
    padded = jnp.concatenate([jnp.zeros((reach_rows, series.shape[1]), jnp.float32), series.astype(jnp.float32)], 0)
    summed = jnp.zeros((length_rows, series.shape[1]), jnp.float32)
    for tap_index in range(kernel.shape[0]):
        summed = summed + kernel[tap_index].astype(jnp.float32) * padded[tap_index:tap_index + length_rows]
    return jax.nn.silu(summed).astype(jnp.bfloat16)

def run_strand(rows_in, segment, w_gate, w_value, w_in_out, w_step, step_bias, decay_rate, skip_gain, conv_value, conv_in_out):
    gate_all = jnp.dot(rows_in, w_gate, preferred_element_type=jnp.float32).astype(jnp.bfloat16)
    value_all = jnp.dot(rows_in, w_value, preferred_element_type=jnp.float32).astype(jnp.bfloat16)
    inout_all = jnp.dot(rows_in, w_in_out, preferred_element_type=jnp.float32).astype(jnp.bfloat16)
    step_raw = jnp.dot(rows_in, w_step, preferred_element_type=jnp.float32)
    values_conv = causal_conv(value_all, conv_value)
    inout_conv = causal_conv(inout_all, conv_in_out)
    step_size = jax.nn.softplus(step_raw + step_bias)
    log_decay = -step_size * decay_rate
    count_spans = LENGTH // SPAN
    span_values = values_conv.reshape(count_spans, SPAN, H, P_SIZE)
    span_inputs = inout_conv[:, :NS].reshape(count_spans, SPAN, NS)
    span_outputs = inout_conv[:, NS:].reshape(count_spans, SPAN, NS)
    span_logs = log_decay.reshape(count_spans, SPAN, H)
    span_steps = step_size.reshape(count_spans, SPAN, H)
    span_segments = segment.reshape(count_spans, SPAN)

    def advance(carried_pair, span_in):
        state_now, segment_last = carried_pair
        values, input_maps, output_maps, logs_here, steps_here, segs_here = span_in
        intra_part, span_state, inflow, passing = span_terms(values, input_maps, output_maps, logs_here, steps_here, segs_here, segment_last)
        entry_state = lax.optimization_barrier(state_now.astype(jnp.bfloat16)).astype(jnp.float32)
        carried = jnp.einsum('in,hpn->ihp', output_maps.astype(jnp.float32), entry_state)
        mixed = intra_part + inflow[:, :, None] * carried + skip_gain[None, :, None] * values.astype(jnp.float32)
        next_state = passing[:, None, None] * state_now + span_state
        return ((next_state, segs_here[-1]), mixed)
    initial = (jnp.zeros((H, P_SIZE, NS), jnp.float32), segment[0])
    ignored_carry, mixed_all = lax.scan(advance, initial, (span_values, span_inputs, span_outputs, span_logs, span_steps, span_segments))
    mixed_all = mixed_all.reshape(LENGTH, H * P_SIZE)
    gate_wide = lax.optimization_barrier(gate_all).astype(jnp.float32)
    gated_out = mixed_all * jax.nn.silu(gate_wide)
    grouped = gated_out.reshape(LENGTH, H // GROUP_HEADS, GROUP_HEADS * P_SIZE)
    normed = grouped * lax.rsqrt(lax.optimization_barrier(jnp.mean(grouped * grouped, axis=2, keepdims=True)) + 1e-05)
    return normed.reshape(LENGTH, H * P_SIZE).astype(jnp.bfloat16)

def reference(hidden, segment_ids, norm_gain, w_gate, w_value, w_in_out, w_step, step_bias, decay_rate, skip_gain, conv_value, conv_in_out, w_out):
    outputs = []
    for window in range(hidden.shape[0]):
        widened = hidden[window].astype(jnp.float32)
        scaled = widened * lax.rsqrt(lax.optimization_barrier(jnp.mean(widened * widened, axis=1, keepdims=True)) + 1e-05)
        forward_in = (scaled * norm_gain).astype(jnp.bfloat16)
        reverse_in = (scaled[::-1, ::-1] * norm_gain).astype(jnp.bfloat16)
        segment = segment_ids[window]
        forward_mix = run_strand(forward_in, segment, w_gate, w_value, w_in_out, w_step, step_bias, decay_rate, skip_gain, conv_value, conv_in_out)
        reverse_mix = run_strand(reverse_in, segment[::-1], w_gate, w_value, w_in_out, w_step, step_bias, decay_rate, skip_gain, conv_value, conv_in_out)
        direct = jnp.dot(forward_mix, w_out, preferred_element_type=jnp.float32)
        flipped = jnp.dot(reverse_mix, w_out, preferred_element_type=jnp.float32)[::-1, ::-1]
        outputs.append((direct + flipped).astype(jnp.bfloat16))
    return jnp.stack(outputs)
```

```python
import functools

import jax
import jax.numpy as jnp
from jax import lax
from jax.experimental import pallas as pl
from jax.experimental.pallas import tpu as pltpu
from jax.sharding import PartitionSpec as P

SPAN = 256
GROUP_HEADS = 8


def with_halo(block, sides, width):
    for axis, dim in sides:
        count = lax.axis_size(axis)
        forward = [(i, i + 1) for i in range(count - 1)]
        backward = [(target, source) for source, target in forward]
        low = lax.ppermute(
            lax.slice_in_dim(block, block.shape[dim] - width, None, axis=dim), axis, forward
        )
        high = lax.ppermute(lax.slice_in_dim(block, 0, width, axis=dim), axis, backward)
        block = jnp.concatenate([low, block, high], axis=dim)
    return block


def passed_along(value, axis, by):
    size = lax.axis_size(axis)
    pairs = [(i, i + by) for i in range(size) if 0 <= i + by < size]
    return lax.ppermute(value, axis, pairs)


def entering(value, axis, combine, identity, reverse):
    size, index = (lax.axis_size(axis), lax.axis_index(axis))
    everything = jax.tree.map(
        lambda part, kind: lax.all_gather(part.astype(kind), axis),
        value,
        (jnp.bfloat16, jnp.bfloat16),
    )
    start = jax.tree.map(
        lambda part, zero: jnp.broadcast_to(jnp.asarray(zero, part.dtype), part.shape),
        value,
        identity,
    )

    def lap(k, before):
        at = size - 1 - k if reverse else k
        reached = at > index if reverse else at < index
        new = combine(
            before, jax.tree.map(lambda part, own: part[at].astype(own.dtype), everything, value)
        )
        return jax.tree.map(lambda a, b: jnp.where(reached, a, b), new, before)

    return lax.fori_loop(0, size, lap, start)


def span_terms(values, input_maps, output_maps, log_decay, step_size, segment, segment_before):
    span_rows = values.shape[0]
    earlier = jnp.tril(jnp.ones((span_rows, span_rows), jnp.float32))
    cumulative = jnp.dot(earlier, log_decay, precision=lax.Precision.HIGHEST)
    scores = jnp.dot(output_maps, input_maps.T, preferred_element_type=jnp.float32)
    row_index = lax.broadcasted_iota(jnp.int32, (span_rows, span_rows), 0)
    col_index = lax.broadcasted_iota(jnp.int32, (span_rows, span_rows), 1)
    allowed = (segment[:, None] == segment[None, :]) & (col_index <= row_index)
    cum_heads = cumulative.T
    spread = cum_heads[:, :, None] - cum_heads[:, None, :]
    weights = jnp.where(allowed[None], jnp.exp(jnp.where(allowed[None], spread, 0.0)), 0.0)
    mixing = (scores[None] * weights * step_size.T[:, None, :]).astype(jnp.bfloat16)
    intra_part = jnp.einsum("hij,jhp->ihp", mixing, values, preferred_element_type=jnp.float32)
    final_cum = cumulative[-1]
    same_end = (segment == segment[-1]).astype(jnp.float32)
    to_end = jnp.exp(final_cum[None] - cumulative) * step_size * same_end[:, None]
    weighted = (values.astype(jnp.float32) * to_end[:, :, None]).astype(jnp.bfloat16)
    span_state = jnp.einsum("jhp,jn->hpn", weighted, input_maps, preferred_element_type=jnp.float32)
    inflow = jnp.exp(cumulative) * (segment == segment_before).astype(jnp.float32)[:, None]
    passing = jnp.exp(final_cum) * (segment[-1] == segment_before).astype(jnp.float32)
    return (intra_part, span_state, inflow, passing)


def causal_conv(series, prior_rows, kernel):
    length_rows = series.shape[1]
    padded = jnp.concatenate([prior_rows, series], 1).astype(jnp.float32)
    summed = jnp.zeros(series.shape, jnp.float32)
    for tap_index in range(kernel.shape[0]):
        summed = (
            summed
            + kernel[tap_index].astype(jnp.float32) * padded[:, tap_index : tap_index + length_rows]
        )
    return jax.nn.silu(summed).astype(jnp.bfloat16)


def normalize(block_rows):
    widened = block_rows.astype(jnp.float32)
    return widened * lax.rsqrt(jnp.mean(widened * widened, axis=1, keepdims=True) + 1e-05)


def combine(earlier_part, later_part):
    return (
        earlier_part[0] * later_part[0],
        later_part[0][..., None, None] * earlier_part[1] + later_part[1],
    )


def compose(carried, inputs_pair):
    state_now, decay_now = carried
    span_state, span_pass = inputs_pair
    return (
        (span_pass[..., None, None] * state_now + span_state, decay_now * span_pass),
        (state_now, decay_now),
    )


def body(
    hidden,
    segment_ids,
    norm_gain,
    w_gate,
    w_value,
    w_in_out,
    w_step,
    step_bias,
    decay_rate,
    skip_gain,
    conv_value,
    conv_in_out,
    w_out,
):
    rows_local = hidden[0]
    segment = segment_ids[0]
    tok_count = rows_local.shape[0]
    extended = with_halo(segment, (("seq", 0),), 1)
    forward_full = lax.all_gather(rows_local, "mp", axis=1, tiled=True)
    reverse_full = forward_full[::-1]
    reverse_edges = extended[::-1]
    forward_in = (normalize(forward_full) * norm_gain).astype(jnp.bfloat16)
    reverse_in = (normalize(reverse_full)[:, ::-1] * norm_gain).astype(jnp.bfloat16)
    both_in = jnp.concatenate([forward_in, reverse_in], 0)
    pieces = (
        lax.all_gather(w_gate, "seq", axis=0, tiled=True),
        lax.all_gather(w_value, "seq", axis=0, tiled=True),
        lax.all_gather(w_in_out, "seq", axis=0, tiled=True),
        lax.all_gather(w_step, "seq", axis=0, tiled=True),
    )
    gate_sum, value_sum, inout_sum, step_sum = tuple(
        (jnp.dot(both_in, weight, preferred_element_type=jnp.float32) for weight in pieces)
    )
    gate_all = gate_sum.astype(jnp.bfloat16).reshape(2, tok_count, -1)
    value_pre = value_sum.astype(jnp.bfloat16).reshape(2, tok_count, -1)
    inout_pre = inout_sum.astype(jnp.bfloat16).reshape(2, tok_count, -1)
    reach_rows = conv_value.shape[0] - 1
    value_tail = value_pre[:, tok_count - reach_rows :]
    inout_tail = inout_pre[:, tok_count - reach_rows :]
    forward_prior = passed_along((value_tail[0], inout_tail[0]), "seq", 1)
    reverse_prior = passed_along((value_tail[1], inout_tail[1]), "seq", -1)
    value_prior = jnp.stack([forward_prior[0], reverse_prior[0]])
    inout_prior = jnp.stack([forward_prior[1], reverse_prior[1]])
    values_conv = causal_conv(value_pre, value_prior, conv_value)
    inout_conv = causal_conv(inout_pre, inout_prior, conv_in_out)
    inout_full = lax.all_gather(inout_conv, "mp", axis=2, tiled=True)
    state_width = inout_full.shape[2] // 2
    step_size = jax.nn.softplus(step_sum.reshape(2, tok_count, -1) + step_bias)
    log_decay = -step_size * decay_rate
    heads_local = step_size.shape[2]
    head_width = values_conv.shape[2] // heads_local
    count_spans = tok_count // SPAN
    segments_pair = jnp.stack([extended[1:-1], reverse_edges[1:-1]]).reshape(2, count_spans, SPAN)
    priors_pair = jnp.stack([extended[0], reverse_edges[0]])
    before_pair = jnp.concatenate([priors_pair[:, None], segments_pair[:, :-1, -1]], 1)
    span_values = values_conv.reshape(2, count_spans, SPAN, heads_local, head_width)
    span_inputs = inout_full[..., :state_width].reshape(2, count_spans, SPAN, state_width)
    span_outputs = inout_full[..., state_width:].reshape(2, count_spans, SPAN, state_width)
    span_logs = log_decay.reshape(2, count_spans, SPAN, heads_local)
    span_steps = step_size.reshape(2, count_spans, SPAN, heads_local)
    intra_part, states, inflow, passing = jax.vmap(jax.vmap(span_terms))(
        span_values, span_inputs, span_outputs, span_logs, span_steps, segments_pair, before_pair
    )
    start_pair = (
        jnp.zeros(states.shape[:1] + states.shape[2:], jnp.float32),
        jnp.ones((2, heads_local), jnp.float32),
    )
    summary_pair, before_parts = lax.scan(
        compose, start_pair, (jnp.moveaxis(states, 1, 0), jnp.moveaxis(passing, 1, 0))
    )
    summary_state, summary_decay = summary_pair
    before_states, before_decay = before_parts
    identity = (jnp.ones_like(summary_decay[0]), jnp.zeros_like(summary_state[0]))
    forward_entry = entering((summary_decay[0], summary_state[0]), "seq", combine, identity, False)
    reverse_entry = entering((summary_decay[1], summary_state[1]), "seq", combine, identity, True)
    entry_state = jnp.stack([forward_entry[1], reverse_entry[1]])
    span_entry = before_states + before_decay[..., None, None] * entry_state[None]
    span_entry = jnp.moveaxis(span_entry, 0, 1).astype(jnp.bfloat16)
    carried = jnp.einsum(
        "skin,skhpn->skihp", span_outputs, span_entry, preferred_element_type=jnp.float32
    )
    mixed = (
        intra_part
        + inflow[..., None] * carried
        + skip_gain[:, None] * span_values.astype(jnp.float32)
    )
    mixed = mixed.reshape(2, tok_count, heads_local * head_width)
    gate_wide = lax.optimization_barrier(gate_all).astype(jnp.float32)
    gated_out = mixed * jax.nn.silu(gate_wide)
    grouped = gated_out.reshape(2, tok_count, -1, GROUP_HEADS * head_width)
    normed = grouped * lax.rsqrt(jnp.mean(grouped * grouped, axis=3, keepdims=True) + 1e-05)
    normed = normed.reshape(2, tok_count, heads_local * head_width).astype(jnp.bfloat16)
    forward_mix = normed[0]
    reverse_mix = normed[1][::-1]
    block_cols = lax.all_gather(w_out, "seq", axis=1, tiled=True)
    direct = jnp.dot(forward_mix, block_cols, preferred_element_type=jnp.float32)
    flipped = jnp.dot(reverse_mix, block_cols, preferred_element_type=jnp.float32)[:, ::-1]
    running = direct
    running = running + flipped
    result = lax.psum_scatter(running, "mp", scatter_dimension=1, tiled=True).astype(jnp.bfloat16)
    return result[None]


MESH = pl.DeviceIdType.MESH
F32 = jnp.float32
BF16 = jnp.bfloat16


def mm(a, b):
    return jnp.dot(a, b, preferred_element_type=F32)


def parts(value, count):
    out = []
    for _ in range(count):
        piece = value.astype(BF16)
        out.append(piece)
        value = value - piece.astype(F32)
    return out


def fused_kernel(
    S,
    heads,
    hidden,
    segs,
    gain,
    w_value,
    w_small,
    w_gate,
    w_out,
    bias,
    rate,
    skip,
    conv,
    out,
    hbuf,
    wv,
    wg,
    wo,
    u,
    pre,
    step,
    gate,
    tsend,
    trecv,
    maps,
    xb,
    smask,
    cs,
    ct,
    dtt,
    seg_col,
    state,
    inflow,
    ein,
    eout,
    mixed,
    mix,
    osend,
    orecv,
    lsem,
    hsem,
    zsend,
    zrecv,
    ysend,
    yrecv,
    csend,
    crecv,
    tsem,
    msem,
    esend,
    erecv,
    osem,
):
    g = lax.axis_index("groups")
    s = lax.axis_index("seq")
    m = lax.axis_index("mp")
    b = lax.axis_index("batch")
    mine, across = g * 2 + b, (1 - g) * 2 + b
    rows = hidden.shape[0]
    half = hidden.shape[1]
    chan = w_value.shape[1]
    depth = w_value.shape[0]
    out_cols = w_out.shape[1]
    to_y, to_core, to_mp = {"groups": 1 - g}, {"batch": 1 - b}, {"mp": 1 - m}

    barrier = pltpu.get_barrier_semaphore()
    for peer in (to_y, to_core, to_mp):
        pl.semaphore_signal(barrier, inc=1, device_id=peer, device_id_type=MESH)

    @pl.when(s > 0)
    def _():
        pl.semaphore_signal(barrier, inc=1, device_id={"seq": s - 1}, device_id_type=MESH)

    @pl.when(s < S - 1)
    def _():
        pl.semaphore_signal(barrier, inc=1, device_id={"seq": s + 1}, device_id_type=MESH)

    own_rows = pl.ds(pl.multiple_of(s * depth, depth), depth)
    local = [
        pltpu.make_async_copy(hidden, hbuf.at[m], lsem.at[0]),
        pltpu.make_async_copy(w_value, wv.at[own_rows, pl.ds(0, chan)], lsem.at[1]),
        pltpu.make_async_copy(w_small, wv.at[own_rows, pl.ds(chan, 256)], lsem.at[2]),
        pltpu.make_async_copy(w_gate, wg.at[own_rows], lsem.at[3]),
        pltpu.make_async_copy(w_out, wo.at[s], lsem.at[4]),
    ]
    for copy in local:
        copy.start()

    lone = jnp.where((s == 0) | (s == S - 1), 1, 0)
    pl.semaphore_wait(barrier, 5 - lone)

    def piece(w, t, quarter):
        if w == 2:
            size = w_out.shape[0] // 4
            return wo.at[t, pl.ds(pl.multiple_of(quarter * size, size), size)]
        size = depth // 4
        start = pl.multiple_of(t * depth + quarter * size, size)
        return (wv, wg)[w].at[pl.ds(start, size)]

    def came(d, k):
        return s - k if d == 0 else s + k

    def comes(d, k):
        return s >= k if d == 0 else s + k <= S - 1

    def z_copy(w, d, k):
        part = piece(w, came(d, k - 1), mine)
        peer = {"seq": s + 1 if d == 0 else s - 1}
        return pltpu.make_async_remote_copy(
            part, part, zsend.at[w, d, k - 1], zrecv.at[w, d, k - 1], peer, MESH
        )

    def z_wait(w, d, k):
        part = piece(w, came(d, k), mine)
        peer = {"seq": s - 1 if d == 0 else s + 1}
        pltpu.make_async_remote_copy(
            part, part, zsend.at[w, d, k - 1], zrecv.at[w, d, k - 1], peer, MESH
        ).wait_recv()

    def sends(d, k):
        held = comes(d, k - 1)
        return held & (s < S - 1) if d == 0 else held & (s > 0)

    def y_copy(w, d, k, quarter):
        part = piece(w, came(d, k), quarter)
        return pltpu.make_async_remote_copy(
            part, part, ysend.at[w, d, k - 1], yrecv.at[w, d, k - 1], to_y, MESH
        )

    def c_copy(w, d, k, which, quarter):
        part = piece(w, came(d, k), quarter)
        return pltpu.make_async_remote_copy(
            part, part, csend.at[w, d, k - 1, which], crecv.at[w, d, k - 1, which], to_core, MESH
        )

    def start_round(w, k):
        for d in (0, 1):

            @pl.when(sends(d, k))
            def _():
                z_copy(w, d, k).start()

    def step_a(w, k):
        for d in (0, 1):

            @pl.when(comes(d, k))
            def _():
                z_wait(w, d, k)
                if k < S - 1:

                    @pl.when(sends(d, k + 1))
                    def _():
                        z_copy(w, d, k + 1).start()

                y_copy(w, d, k, mine).start()
                c_copy(w, d, k, 0, mine).start()

    def step_b(w, k):
        for d in (0, 1):

            @pl.when(comes(d, k))
            def _():
                y_copy(w, d, k, across).wait_recv()
                c_copy(w, d, k, 1, across).start()

    def step_c(w):
        other = g * 2 + 1 - b
        other_across = (1 - g) * 2 + 1 - b
        for k in range(1, S):
            for d in (0, 1):

                @pl.when(comes(d, k))
                def _():
                    c_copy(w, d, k, 0, other).wait_recv()
                    c_copy(w, d, k, 1, other_across).wait_recv()

    def settle():
        for w in range(3):
            for k in range(1, S):
                for d in (0, 1):

                    @pl.when(sends(d, k))
                    def _():
                        z_copy(w, d, k).wait_send()

                    @pl.when(comes(d, k))
                    def _():
                        y_copy(w, d, k, mine).wait_send()
                        c_copy(w, d, k, 0, mine).wait_send()
                        c_copy(w, d, k, 1, across).wait_send()

    local[1].wait()
    local[2].wait()
    start_round(0, 1)
    local[0].wait()
    h_copy = pltpu.make_async_remote_copy(
        hbuf.at[m], hbuf.at[m], hsem.at[0], hsem.at[1], to_mp, MESH
    )
    h_copy.start()
    local[3].wait()
    start_round(1, 1)
    local[4].wait()

    ri = lax.broadcasted_iota(jnp.int32, (rows, rows), 0)
    ci = lax.broadcasted_iota(jnp.int32, (rows, rows), 1)
    eye = ri == ci
    anti = ri + ci == rows - 1
    flip = jnp.where(anti, 1.0, 0.0).astype(BF16)
    lower = jnp.where(ci <= ri, 1.0, 0.0).astype(BF16)

    def turned(row, where):
        return jnp.sum(jnp.where(where, row, 0.0), axis=1, keepdims=True)

    seg_row = segs[...].astype(F32)
    seg_c = turned(seg_row, eye)
    seg_c_rev = turned(seg_row, anti)
    seg_row_rev = jnp.sum(jnp.where(anti, seg_c, 0.0), axis=0, keepdims=True)
    strand_rows = (seg_row, seg_row_rev)
    strand_cols = (seg_c, seg_c_rev)
    for st in (0, 1):
        seg_col[st] = jnp.broadcast_to(strand_cols[st], (rows, 128))

    step_a(0, 1)
    step_a(1, 1)
    step_b(0, 1)
    pltpu.make_async_remote_copy(
        hbuf.at[1 - m], hbuf.at[1 - m], hsem.at[0], hsem.at[1], to_mp, MESH
    ).wait_recv()

    total = jnp.zeros((rows, 1), F32)
    for i in range(2):
        wide = hbuf[i].astype(F32)
        total = total + jnp.sum(wide * wide, axis=1, keepdims=True)
    inv = lax.rsqrt(total / (2 * half) + 1e-05)
    inv_row = jnp.sum(jnp.where(eye, inv, 0.0), axis=0, keepdims=True)
    inv_rev = turned(inv_row, anti)
    blocks = half // 256
    for i in range(2 * blocks):
        there = pl.ds(i * 256, 256)
        back = pl.ds((2 * blocks - 1 - i) * 256, 256)
        block = hbuf[i // blocks, :, (i % blocks) * 256 : (i % blocks + 1) * 256]
        u[0:rows, there] = ((block.astype(F32) * inv) * gain[:, there]).astype(BF16)
        turned_block = mm(mm(flip, block).astype(BF16), flip)
        u[rows : 2 * rows, back] = ((turned_block * inv_rev) * gain[:, back]).astype(BF16)

    step_a(0, 2)
    step_b(1, 1)
    step_a(1, 2)
    step_b(0, 2)
    step_a(0, 3)
    start_round(2, 1)
    step_b(1, 2)
    step_b(0, 3)
    step_c(0)

    small = mm(u[...], wv[:, chan : chan + 256])
    for st in (0, 1):
        pre[st, 8 : 8 + rows, chan : chan + 128] = (
            small[st * rows : (st + 1) * rows, :128].astype(BF16).astype(F32)
        )
        step[st] = small[st * rows : (st + 1) * rows, 128:]

    @pl.loop(0, chan // 256)
    def _(n):
        cols = pl.ds(pl.multiple_of(n * 256, 256), 256)
        got = mm(u[...], wv[:, cols]).astype(BF16).astype(F32)
        for st in (0, 1):
            pre[st, 8 : 8 + rows, cols] = got[st * rows : (st + 1) * rows]

    def has_next(st):
        return s < S - 1 if st == 0 else s > 0

    def has_prev(st):
        return s > 0 if st == 0 else s < S - 1

    def t_copy(st):
        peer = {"seq": s + 1 if st == 0 else s - 1}
        return pltpu.make_async_remote_copy(
            tsend.at[st], trecv.at[st], tsem.at[0, st], tsem.at[1, st], peer, MESH
        )

    for st in (0, 1):
        tsend[st, :, 0 : chan + 128] = pre[st, rows - 8 : rows + 8, :].astype(BF16)
        tsend[st, :, chan + 128 : chan + 256] = seg_col[st, rows - 16 : rows, :].astype(BF16)

        @pl.when(has_next(st))
        def _():
            t_copy(st).start()

    step_a(2, 1)
    step_a(1, 3)
    for st in (0, 1):
        raw = step[st] + bias[...]
        dt = jnp.maximum(raw, 0.0) + jnp.log1p(jnp.exp(-jnp.abs(raw)))
        decay = -dt * rate[...]
        c = sum(mm(lower, p) for p in parts(decay, 3))
        cs[st] = c
        ct[st] = c.T
        dtt[st] = dt.T
        last = c[rows - 1 : rows, :]
        end = strand_cols[st][rows - 1 : rows, :]
        step[st] = jnp.exp(last - c) * dt * jnp.where(strand_cols[st] == end, 1.0, 0.0)

    for st in (0, 1):

        @pl.when(has_prev(st))
        def _():
            t_copy(st).wait_recv()
            pre[st, 0:8, :] = trecv[st, 8:16, 0 : chan + 128].astype(F32)
            seg_col[st + 2, 0:8, :] = trecv[st, 8:16, chan + 128 : chan + 256].astype(F32)

        @pl.when(jnp.logical_not(has_prev(st)))
        def _():
            pre[st, 0:8, :] = jnp.zeros((8, chan + 128), F32)
            seg_col[st + 2, 0:8, :] = seg_col[st, 0:8, :]

    def convolved(st, cols):
        total = jnp.zeros((rows, cols.size), F32)
        for k in range(4):
            total = total + conv[k : k + 1, cols] * pre[st, 5 + k : 5 + k + rows, cols]
        return (total * jax.nn.sigmoid(total)).astype(BF16)

    m_copy = pltpu.make_async_remote_copy(
        maps.at[m], maps.at[m], msem.at[0], msem.at[1], to_mp, MESH
    )
    for st in (0, 1):
        maps[m, st] = convolved(st, pl.ds(chan, 128))
    m_copy.start()

    step_b(2, 1)

    @pl.loop(0, chan // 128)
    def _(n):
        cols = pl.ds(pl.multiple_of(n * 128, 128), 128)
        for st in (0, 1):
            xb[st, :, cols] = convolved(st, cols)

    step_a(2, 2)
    step_b(1, 3)
    pltpu.make_async_remote_copy(
        maps.at[1 - m], maps.at[1 - m], msem.at[0], msem.at[1], to_mp, MESH
    ).wait_recv()

    hrow = lax.broadcasted_iota(jnp.int32, (128, chan), 0)
    hcol = lax.broadcasted_iota(jnp.int32, (128, chan), 1)
    width = chan // heads
    spread = jnp.where(hcol // width == hrow, 1.0, 0.0).astype(BF16)

    def widened(value):
        return sum(mm(p, spread) for p in parts(value, 2))

    passing = []
    for st in (0, 1):
        b_map, c_map = maps[0, st], maps[1, st]
        scores = lax.dot_general(
            c_map, b_map, (((1,), (1,)), ((), ())), preferred_element_type=F32
        )
        allowed = (strand_cols[st] == strand_rows[st]) & (ci <= ri)
        smask[st] = jnp.where(allowed, scores, 0.0)
        weighted = (xb[st].astype(F32) * widened(step[st])).astype(BF16)
        state[st] = mm(b_map.astype(F32).T.astype(BF16), weighted)
        before = seg_col[st + 2, 7:8, 0:1]
        c = cs[st]
        flow = jnp.exp(c) * jnp.where(strand_cols[st] == before, 1.0, 0.0)
        inflow[st] = flow
        passing.append(widened(flow[rows - 8 : rows])[7:8])

    def e_copy(st, n):
        cols = pl.ds(n * 512, 512)
        peer = {"seq": s + 1 if st == 0 else s - 1}
        return pltpu.make_async_remote_copy(
            eout.at[st, :, cols], ein.at[st, :, cols], esend.at[st, n], erecv.at[st, n], peer, MESH
        )

    def hop(st, n):
        cols = slice(n * 512, (n + 1) * 512)

        @pl.when(has_prev(st))
        def _():
            e_copy(st, n).wait_recv()

        @pl.when(jnp.logical_not(has_prev(st)))
        def _():
            ein[st, :, cols] = jnp.zeros((128, 512), BF16)

        @pl.when(has_next(st))
        def _():
            eout[st, :, cols] = (
                passing[st][:, cols] * ein[st, :, cols].astype(F32) + state[st, :, cols]
            ).astype(BF16)
            e_copy(st, n).start()

    chunks = chan // 512

    def first_hops():
        for n in range(chunks):
            for st in (0, 1):

                @pl.when(jnp.logical_not(has_prev(st)))
                def _():
                    hop_now(st, n)

    def hop_now(st, n):
        cols = slice(n * 512, (n + 1) * 512)
        ein[st, :, cols] = jnp.zeros((128, 512), BF16)
        eout[st, :, cols] = state[st, :, cols].astype(BF16)
        e_copy(st, n).start()

    first_hops()

    pairs = chan // 128
    lane = lax.broadcasted_iota(jnp.int32, (rows, 128), 1)

    def intra(i):
        st, q = i // pairs, i % pairs
        cols = pl.ds(pl.multiple_of(q * 128, 128), 128)
        x_pair = xb[st, :, cols]
        sm = smask[st]
        c_all = cs[st]
        got = []
        for e in (0, 1):
            h = 2 * q + e
            c_col = pltpu.roll(c_all, (128 - h) % 128, 1)[:, 0:1]
            c_row = ct[st, pl.ds(h, 1), :]
            dt_row = dtt[st, pl.ds(h, 1), :]
            mixing = sm * jnp.exp(jnp.minimum(c_col - c_row, 0.0)) * dt_row
            got.append(mm(mixing.astype(BF16), x_pair))
        mixed[st, :, cols] = jnp.where(lane < width, got[0], got[1])

    def intra_range(lo, hi):
        @pl.loop(lo, hi)
        def _(i):
            intra(i)

    def later_hops(low_strand):
        for n in range(chunks):
            for near in (0, 1):
                st = near if low_strand else 1 - near

                @pl.when(has_prev(st))
                def _():
                    hop(st, n)

    intra_range(0, pairs)

    @pl.when(s < S // 2)
    def _():
        later_hops(True)

    @pl.when(s >= S // 2)
    def _():
        later_hops(False)

    step_a(2, 3)
    step_b(2, 2)
    intra_range(pairs, 2 * pairs)
    step_b(2, 3)
    step_c(1)

    @pl.loop(0, chan // 256)
    def _(n):
        cols = pl.ds(pl.multiple_of(n * 256, 256), 256)
        got = mm(u[...], wg[:, cols]).astype(BF16)
        for st in (0, 1):
            gate[st, :, cols] = got[st * rows : (st + 1) * rows]

    group = GROUP_HEADS * width
    for st in (0, 1):
        for n in range(chan // group):
            cols = slice(n * group, (n + 1) * group)
            flow = sum(mm(p, spread[:, cols]) for p in parts(inflow[st], 2))
            value = (
                mixed[st, :, cols]
                + flow * mm(maps[1, st], ein[st, :, cols])
                + skip[:, cols] * xb[st, :, cols].astype(F32)
            )
            wide = gate[st, :, cols].astype(F32)
            value = value * (wide * jax.nn.sigmoid(wide))
            scale = lax.rsqrt(jnp.mean(value * value, axis=1, keepdims=True) + 1e-05)
            normed = (value * scale).astype(BF16)
            if st == 1:
                normed = mm(flip, normed).astype(BF16)
            mix[st, :, cols] = normed

    step_c(2)
    per_half = S // 2

    def columns(t):
        direct = mm(mix[0], wo[t])
        turned_part = mm(mix[1], wo[S - 1 - t])
        count = out_cols // 256
        flipped = []
        for i in range(count):
            at = count - 1 - i
            flipped.append(
                sum(mm(p, flip) for p in parts(turned_part[:, at * 256 : (at + 1) * 256], 2))
            )
        return direct + jnp.concatenate(flipped, axis=1)

    def o_copy(i):
        return pltpu.make_async_remote_copy(
            osend.at[i], orecv.at[i], osem.at[0, i], osem.at[1, i], to_mp, MESH
        )

    for i in range(per_half):
        osend[i] = columns((1 - m) * per_half + i).astype(BF16)
        o_copy(i).start()
    for i in range(per_half):
        own = columns(m * per_half + i)
        o_copy(i).wait_recv()
        out[:, i * out_cols : (i + 1) * out_cols] = (own + orecv[i].astype(F32)).astype(BF16)

    settle()
    h_copy.wait_send()
    m_copy.wait_send()
    for st in (0, 1):

        @pl.when(has_next(st))
        def _():
            t_copy(st).wait_send()
            for n in range(chunks):
                e_copy(st, n).wait_send()

    for i in range(per_half):
        o_copy(i).wait_send()


def fused_body(
    hidden,
    segment_ids,
    norm_gain,
    w_gate,
    w_value,
    w_in_out,
    w_step,
    step_bias,
    decay_rate,
    skip_gain,
    conv_value,
    conv_in_out,
    w_out,
):
    S = lax.axis_size("seq")
    rows, half = hidden.shape[1:]
    depth, chan = w_value.shape
    heads = w_step.shape[1]
    maps_width = w_in_out.shape[1]
    out_cols = w_out.shape[1]
    padded = 128 - heads
    w_small = jnp.concatenate([w_in_out, jnp.pad(w_step, ((0, 0), (0, padded)))], axis=1)
    bias = jnp.pad(step_bias, (0, padded))[None]
    rate = jnp.pad(decay_rate, (0, padded))[None]
    skip = jnp.repeat(skip_gain, chan // heads)[None]
    conv = jnp.concatenate([conv_value, conv_in_out], axis=1).astype(F32)
    conv = jnp.pad(conv, ((0, 4), (0, 0)))
    anywhere = pl.BlockSpec(memory_space=pl.ANY)
    vmem = pl.BlockSpec(memory_space=pltpu.VMEM)
    dma = pltpu.SemaphoreType.DMA
    result = pl.pallas_call(
        functools.partial(fused_kernel, S, heads),
        out_shape=jax.ShapeDtypeStruct((rows, half), BF16),
        in_specs=[anywhere, vmem, vmem] + [anywhere] * 4 + [vmem] * 4,
        out_specs=vmem,
        scratch_shapes=[
            pltpu.VMEM((2, rows, half), BF16),
            pltpu.VMEM((S * depth, chan + 256), BF16),
            pltpu.VMEM((S * depth, chan), BF16),
            pltpu.VMEM((S, chan, out_cols), BF16),
            pltpu.VMEM((2 * rows, 2 * half), BF16),
            pltpu.VMEM((2, rows + 8, chan + maps_width), F32),
            pltpu.VMEM((2, rows, 128), F32),
            pltpu.VMEM((2, rows, chan), BF16),
            pltpu.VMEM((2, 16, chan + 256), BF16),
            pltpu.VMEM((2, 16, chan + 256), BF16),
            pltpu.VMEM((2, 2, rows, maps_width), BF16),
            pltpu.VMEM((2, rows, chan), BF16),
            pltpu.VMEM((2, rows, rows), F32),
            pltpu.VMEM((2, rows, 128), F32),
            pltpu.VMEM((2, 128, rows), F32),
            pltpu.VMEM((2, 128, rows), F32),
            pltpu.VMEM((4, rows, 128), F32),
            pltpu.VMEM((2, 128, chan), F32),
            pltpu.VMEM((2, rows, 128), F32),
            pltpu.VMEM((2, 128, chan), BF16),
            pltpu.VMEM((2, 128, chan), BF16),
            pltpu.VMEM((2, rows, chan), F32),
            pltpu.VMEM((2, rows, chan), BF16),
            pltpu.VMEM((S // 2, rows, out_cols), BF16),
            pltpu.VMEM((S // 2, rows, out_cols), BF16),
            dma((5,)),
            dma((2,)),
            dma((3, 2, S - 1)),
            dma((3, 2, S - 1)),
            dma((3, 2, S - 1)),
            dma((3, 2, S - 1)),
            dma((3, 2, S - 1, 2)),
            dma((3, 2, S - 1, 2)),
            dma((2, 2)),
            dma((2,)),
            dma((2, chan // 512)),
            dma((2, chan // 512)),
            dma((2, S // 2)),
        ],
        compiler_params=pltpu.CompilerParams(
            collective_id=0, has_side_effects=True, vmem_limit_bytes=56 * 2**20
        ),
        name="fused",
    )(
        hidden[0],
        segment_ids,
        norm_gain[None],
        w_value,
        w_small,
        w_gate,
        w_out,
        bias,
        rate,
        skip,
        conv,
    )
    return result[None]


def solution(mesh):
    placed = (
        P(("groups", "batch"), "seq", "mp"),
        P(("groups", "batch"), "seq"),
        P(),
        P("seq", "mp"),
        P("seq", "mp"),
        P("seq", "mp"),
        P("seq", "mp"),
        P("mp"),
        P("mp"),
        P("mp"),
        P(None, "mp"),
        P(None, "mp"),
        P("mp", "seq"),
    )
    sizes = mesh.shape
    fits = sizes["mp"] == 2 and sizes["groups"] == 2 and sizes["batch"] == 2
    chosen = fused_body if fits and sizes["seq"] == 4 else body
    return jax.shard_map(
        chosen,
        mesh=mesh,
        in_specs=placed,
        out_specs=P(("groups", "batch"), "seq", "mp"),
        check_vma=False,
    )
```

```python
import functools

import jax
import jax.numpy as jnp
from jax import lax
from jax.experimental import pallas as pl
from jax.experimental.pallas import tpu as pltpu
from jax.sharding import PartitionSpec as P

SPAN = 256
GROUP_HEADS = 8


def with_halo(block, sides, width):
    for axis, dim in sides:
        count = lax.axis_size(axis)
        forward = [(i, i + 1) for i in range(count - 1)]
        backward = [(target, source) for source, target in forward]
        low = lax.ppermute(
            lax.slice_in_dim(block, block.shape[dim] - width, None, axis=dim), axis, forward
        )
        high = lax.ppermute(lax.slice_in_dim(block, 0, width, axis=dim), axis, backward)
        block = jnp.concatenate([low, block, high], axis=dim)
    return block


def passed_along(value, axis, by):
    size = lax.axis_size(axis)
    pairs = [(i, i + by) for i in range(size) if 0 <= i + by < size]
    return lax.ppermute(value, axis, pairs)


def entering(value, axis, combine, identity, reverse):
    size, index = (lax.axis_size(axis), lax.axis_index(axis))
    everything = jax.tree.map(
        lambda part, kind: lax.all_gather(part.astype(kind), axis),
        value,
        (jnp.bfloat16, jnp.bfloat16),
    )
    start = jax.tree.map(
        lambda part, zero: jnp.broadcast_to(jnp.asarray(zero, part.dtype), part.shape),
        value,
        identity,
    )

    def lap(k, before):
        at = size - 1 - k if reverse else k
        reached = at > index if reverse else at < index
        new = combine(
            before, jax.tree.map(lambda part, own: part[at].astype(own.dtype), everything, value)
        )
        return jax.tree.map(lambda a, b: jnp.where(reached, a, b), new, before)

    return lax.fori_loop(0, size, lap, start)


def span_terms(values, input_maps, output_maps, log_decay, step_size, segment, segment_before):
    span_rows = values.shape[0]
    earlier = jnp.tril(jnp.ones((span_rows, span_rows), jnp.float32))
    cumulative = jnp.dot(earlier, log_decay, precision=lax.Precision.HIGHEST)
    scores = jnp.dot(output_maps, input_maps.T, preferred_element_type=jnp.float32)
    row_index = lax.broadcasted_iota(jnp.int32, (span_rows, span_rows), 0)
    col_index = lax.broadcasted_iota(jnp.int32, (span_rows, span_rows), 1)
    allowed = (segment[:, None] == segment[None, :]) & (col_index <= row_index)
    cum_heads = cumulative.T
    spread = cum_heads[:, :, None] - cum_heads[:, None, :]
    weights = jnp.where(allowed[None], jnp.exp(jnp.where(allowed[None], spread, 0.0)), 0.0)
    mixing = (scores[None] * weights * step_size.T[:, None, :]).astype(jnp.bfloat16)
    intra_part = jnp.einsum("hij,jhp->ihp", mixing, values, preferred_element_type=jnp.float32)
    final_cum = cumulative[-1]
    same_end = (segment == segment[-1]).astype(jnp.float32)
    to_end = jnp.exp(final_cum[None] - cumulative) * step_size * same_end[:, None]
    weighted = (values.astype(jnp.float32) * to_end[:, :, None]).astype(jnp.bfloat16)
    span_state = jnp.einsum("jhp,jn->hpn", weighted, input_maps, preferred_element_type=jnp.float32)
    inflow = jnp.exp(cumulative) * (segment == segment_before).astype(jnp.float32)[:, None]
    passing = jnp.exp(final_cum) * (segment[-1] == segment_before).astype(jnp.float32)
    return (intra_part, span_state, inflow, passing)


def causal_conv(series, prior_rows, kernel):
    length_rows = series.shape[1]
    padded = jnp.concatenate([prior_rows, series], 1).astype(jnp.float32)
    summed = jnp.zeros(series.shape, jnp.float32)
    for tap_index in range(kernel.shape[0]):
        summed = (
            summed
            + kernel[tap_index].astype(jnp.float32) * padded[:, tap_index : tap_index + length_rows]
        )
    return jax.nn.silu(summed).astype(jnp.bfloat16)


def normalize(block_rows):
    widened = block_rows.astype(jnp.float32)
    return widened * lax.rsqrt(jnp.mean(widened * widened, axis=1, keepdims=True) + 1e-05)


def combine(earlier_part, later_part):
    return (
        earlier_part[0] * later_part[0],
        later_part[0][..., None, None] * earlier_part[1] + later_part[1],
    )


def compose(carried, inputs_pair):
    state_now, decay_now = carried
    span_state, span_pass = inputs_pair
    return (
        (span_pass[..., None, None] * state_now + span_state, decay_now * span_pass),
        (state_now, decay_now),
    )


def body(
    hidden,
    segment_ids,
    norm_gain,
    w_gate,
    w_value,
    w_in_out,
    w_step,
    step_bias,
    decay_rate,
    skip_gain,
    conv_value,
    conv_in_out,
    w_out,
):
    rows_local = hidden[0]
    segment = segment_ids[0]
    tok_count = rows_local.shape[0]
    extended = with_halo(segment, (("seq", 0),), 1)
    forward_full = lax.all_gather(rows_local, "mp", axis=1, tiled=True)
    reverse_full = forward_full[::-1]
    reverse_edges = extended[::-1]
    forward_in = (normalize(forward_full) * norm_gain).astype(jnp.bfloat16)
    reverse_in = (normalize(reverse_full)[:, ::-1] * norm_gain).astype(jnp.bfloat16)
    both_in = jnp.concatenate([forward_in, reverse_in], 0)
    pieces = (
        lax.all_gather(w_gate, "seq", axis=0, tiled=True),
        lax.all_gather(w_value, "seq", axis=0, tiled=True),
        lax.all_gather(w_in_out, "seq", axis=0, tiled=True),
        lax.all_gather(w_step, "seq", axis=0, tiled=True),
    )
    gate_sum, value_sum, inout_sum, step_sum = tuple(
        (jnp.dot(both_in, weight, preferred_element_type=jnp.float32) for weight in pieces)
    )
    gate_all = gate_sum.astype(jnp.bfloat16).reshape(2, tok_count, -1)
    value_pre = value_sum.astype(jnp.bfloat16).reshape(2, tok_count, -1)
    inout_pre = inout_sum.astype(jnp.bfloat16).reshape(2, tok_count, -1)
    reach_rows = conv_value.shape[0] - 1
    value_tail = value_pre[:, tok_count - reach_rows :]
    inout_tail = inout_pre[:, tok_count - reach_rows :]
    forward_prior = passed_along((value_tail[0], inout_tail[0]), "seq", 1)
    reverse_prior = passed_along((value_tail[1], inout_tail[1]), "seq", -1)
    value_prior = jnp.stack([forward_prior[0], reverse_prior[0]])
    inout_prior = jnp.stack([forward_prior[1], reverse_prior[1]])
    values_conv = causal_conv(value_pre, value_prior, conv_value)
    inout_conv = causal_conv(inout_pre, inout_prior, conv_in_out)
    inout_full = lax.all_gather(inout_conv, "mp", axis=2, tiled=True)
    state_width = inout_full.shape[2] // 2
    step_size = jax.nn.softplus(step_sum.reshape(2, tok_count, -1) + step_bias)
    log_decay = -step_size * decay_rate
    heads_local = step_size.shape[2]
    head_width = values_conv.shape[2] // heads_local
    count_spans = tok_count // SPAN
    segments_pair = jnp.stack([extended[1:-1], reverse_edges[1:-1]]).reshape(2, count_spans, SPAN)
    priors_pair = jnp.stack([extended[0], reverse_edges[0]])
    before_pair = jnp.concatenate([priors_pair[:, None], segments_pair[:, :-1, -1]], 1)
    span_values = values_conv.reshape(2, count_spans, SPAN, heads_local, head_width)
    span_inputs = inout_full[..., :state_width].reshape(2, count_spans, SPAN, state_width)
    span_outputs = inout_full[..., state_width:].reshape(2, count_spans, SPAN, state_width)
    span_logs = log_decay.reshape(2, count_spans, SPAN, heads_local)
    span_steps = step_size.reshape(2, count_spans, SPAN, heads_local)
    intra_part, states, inflow, passing = jax.vmap(jax.vmap(span_terms))(
        span_values, span_inputs, span_outputs, span_logs, span_steps, segments_pair, before_pair
    )
    start_pair = (
        jnp.zeros(states.shape[:1] + states.shape[2:], jnp.float32),
        jnp.ones((2, heads_local), jnp.float32),
    )
    summary_pair, before_parts = lax.scan(
        compose, start_pair, (jnp.moveaxis(states, 1, 0), jnp.moveaxis(passing, 1, 0))
    )
    summary_state, summary_decay = summary_pair
    before_states, before_decay = before_parts
    identity = (jnp.ones_like(summary_decay[0]), jnp.zeros_like(summary_state[0]))
    forward_entry = entering((summary_decay[0], summary_state[0]), "seq", combine, identity, False)
    reverse_entry = entering((summary_decay[1], summary_state[1]), "seq", combine, identity, True)
    entry_state = jnp.stack([forward_entry[1], reverse_entry[1]])
    span_entry = before_states + before_decay[..., None, None] * entry_state[None]
    span_entry = jnp.moveaxis(span_entry, 0, 1).astype(jnp.bfloat16)
    carried = jnp.einsum(
        "skin,skhpn->skihp", span_outputs, span_entry, preferred_element_type=jnp.float32
    )
    mixed = (
        intra_part
        + inflow[..., None] * carried
        + skip_gain[:, None] * span_values.astype(jnp.float32)
    )
    mixed = mixed.reshape(2, tok_count, heads_local * head_width)
    gate_wide = lax.optimization_barrier(gate_all).astype(jnp.float32)
    gated_out = mixed * jax.nn.silu(gate_wide)
    grouped = gated_out.reshape(2, tok_count, -1, GROUP_HEADS * head_width)
    normed = grouped * lax.rsqrt(jnp.mean(grouped * grouped, axis=3, keepdims=True) + 1e-05)
    normed = normed.reshape(2, tok_count, heads_local * head_width).astype(jnp.bfloat16)
    forward_mix = normed[0]
    reverse_mix = normed[1][::-1]
    block_cols = lax.all_gather(w_out, "seq", axis=1, tiled=True)
    direct = jnp.dot(forward_mix, block_cols, preferred_element_type=jnp.float32)
    flipped = jnp.dot(reverse_mix, block_cols, preferred_element_type=jnp.float32)[:, ::-1]
    running = direct
    running = running + flipped
    result = lax.psum_scatter(running, "mp", scatter_dimension=1, tiled=True).astype(jnp.bfloat16)
    return result[None]


MESH = pl.DeviceIdType.MESH
F32 = jnp.float32
BF16 = jnp.bfloat16


def mm(a, b):
    return jnp.dot(a, b, preferred_element_type=F32)


def parts(value, count):
    out = []
    for _ in range(count):
        piece = value.astype(BF16)
        out.append(piece)
        value = value - piece.astype(F32)
    return out


def fused_kernel(
    S,
    heads,
    hidden,
    segs,
    gain,
    w_value,
    w_in_out,
    w_gate,
    w_out,
    step_rows,
    bias_in,
    rate_in,
    skip_in,
    conv_value,
    conv_maps,
    out,
    hbuf,
    wv,
    wg,
    wo,
    u,
    pre,
    step,
    gate,
    tsend,
    trecv,
    maps,
    xb,
    smask,
    cs,
    ct,
    dtt,
    seg_col,
    state,
    inflow,
    ein,
    eout,
    mixed,
    mix,
    osend,
    orecv,
    conv,
    skip,
    lsem,
    hsem,
    zsend,
    zrecv,
    ysend,
    yrecv,
    csend,
    crecv,
    tsem,
    msem,
    esend,
    erecv,
    osem,
):
    g = lax.axis_index("groups")
    s = lax.axis_index("seq")
    m = lax.axis_index("mp")
    b = lax.axis_index("batch")
    mine, across = g * 2 + b, (1 - g) * 2 + b
    rows = hidden.shape[0]
    half = hidden.shape[1]
    chan = w_value.shape[1]
    depth = w_value.shape[0]
    out_cols = w_out.shape[1]
    to_y, to_core, to_mp = {"groups": 1 - g}, {"batch": 1 - b}, {"mp": 1 - m}

    barrier = pltpu.get_barrier_semaphore()
    for peer in (to_y, to_core, to_mp):
        pl.semaphore_signal(barrier, inc=1, device_id=peer, device_id_type=MESH)

    @pl.when(s > 0)
    def _():
        pl.semaphore_signal(barrier, inc=1, device_id={"seq": s - 1}, device_id_type=MESH)

    @pl.when(s < S - 1)
    def _():
        pl.semaphore_signal(barrier, inc=1, device_id={"seq": s + 1}, device_id_type=MESH)

    own_rows = pl.ds(pl.multiple_of(s * depth, depth), depth)
    local = [
        pltpu.make_async_copy(hidden, hbuf.at[m], lsem.at[0]),
        pltpu.make_async_copy(w_value, wv.at[own_rows, pl.ds(0, chan)], lsem.at[1]),
        pltpu.make_async_copy(w_in_out, wv.at[own_rows, pl.ds(chan, 128)], lsem.at[2]),
        pltpu.make_async_copy(w_gate, wg.at[own_rows], lsem.at[3]),
        pltpu.make_async_copy(w_out, wo.at[s], lsem.at[4]),
    ]
    for copy in local:
        copy.start()
    padding = jnp.zeros((128 - heads, depth), F32)
    step_all = jnp.concatenate([step_rows[...].astype(F32), padding], axis=0)
    wv[own_rows, chan + 128 : chan + 256] = step_all.T.astype(BF16)

    def lanes(ref):
        return jnp.concatenate([ref[...], jnp.zeros((1, 128 - heads), F32)], axis=1)

    conv[0:4, 0:chan] = conv_value[...].astype(F32)
    conv[0:4, chan : chan + 128] = conv_maps[...].astype(F32)

    lone = jnp.where((s == 0) | (s == S - 1), 1, 0)
    pl.semaphore_wait(barrier, 5 - lone)

    def piece(w, t, quarter):
        if w >= 2:
            size = w_out.shape[0] // 8
            start = ((w - 2) * 4 + quarter) * size
            return wo.at[t, pl.ds(pl.multiple_of(start, size), size)]
        size = depth // 4
        start = pl.multiple_of(t * depth + quarter * size, size)
        return (wv, wg)[w].at[pl.ds(start, size)]

    def came(d, k):
        return s - k if d == 0 else s + k

    def comes(d, k):
        return s >= k if d == 0 else s + k <= S - 1

    def z_copy(w, d, k):
        part = piece(w, came(d, k - 1), mine)
        peer = {"seq": s + 1 if d == 0 else s - 1}
        return pltpu.make_async_remote_copy(
            part, part, zsend.at[w, d, k - 1], zrecv.at[w, d, k - 1], peer, MESH
        )

    def z_wait(w, d, k):
        part = piece(w, came(d, k), mine)
        peer = {"seq": s - 1 if d == 0 else s + 1}
        pltpu.make_async_remote_copy(
            part, part, zsend.at[w, d, k - 1], zrecv.at[w, d, k - 1], peer, MESH
        ).wait_recv()

    def sends(d, k):
        held = comes(d, k - 1)
        return held & (s < S - 1) if d == 0 else held & (s > 0)

    def y_copy(w, d, k, quarter):
        part = piece(w, came(d, k), quarter)
        return pltpu.make_async_remote_copy(
            part, part, ysend.at[w, d, k - 1], yrecv.at[w, d, k - 1], to_y, MESH
        )

    def c_copy(w, d, k, which, quarter):
        part = piece(w, came(d, k), quarter)
        return pltpu.make_async_remote_copy(
            part, part, csend.at[w, d, k - 1, which], crecv.at[w, d, k - 1, which], to_core, MESH
        )

    def start_round(w, k):
        for d in (0, 1):

            @pl.when(sends(d, k))
            def _():
                z_copy(w, d, k).start()

    def step_a(w, k):
        for d in (0, 1):

            @pl.when(comes(d, k))
            def _():
                z_wait(w, d, k)
                if k < S - 1:

                    @pl.when(sends(d, k + 1))
                    def _():
                        z_copy(w, d, k + 1).start()

                y_copy(w, d, k, mine).start()
                c_copy(w, d, k, 0, mine).start()

    def step_b(w, k):
        for d in (0, 1):

            @pl.when(comes(d, k))
            def _():
                y_copy(w, d, k, across).wait_recv()
                c_copy(w, d, k, 1, across).start()

    def step_c(w, rounds=range(1, S)):
        other = g * 2 + 1 - b
        other_across = (1 - g) * 2 + 1 - b
        for k in rounds:
            for d in (0, 1):

                @pl.when(comes(d, k))
                def _():
                    c_copy(w, d, k, 0, other).wait_recv()
                    c_copy(w, d, k, 1, other_across).wait_recv()

    def settle():
        for w in range(4):
            for k in range(1, S):
                for d in (0, 1):

                    @pl.when(sends(d, k))
                    def _():
                        z_copy(w, d, k).wait_send()

                    @pl.when(comes(d, k))
                    def _():
                        y_copy(w, d, k, mine).wait_send()
                        c_copy(w, d, k, 0, mine).wait_send()
                        c_copy(w, d, k, 1, across).wait_send()

    local[1].wait()
    local[2].wait()
    start_round(0, 1)
    local[0].wait()
    h_copy = pltpu.make_async_remote_copy(
        hbuf.at[m], hbuf.at[m], hsem.at[0], hsem.at[1], to_mp, MESH
    )
    h_copy.start()
    local[3].wait()
    start_round(1, 1)
    local[4].wait()

    ri = lax.broadcasted_iota(jnp.int32, (rows, rows), 0)
    ci = lax.broadcasted_iota(jnp.int32, (rows, rows), 1)
    eye = ri == ci
    anti = ri + ci == rows - 1
    flip = jnp.where(anti, 1.0, 0.0).astype(BF16)
    lower = jnp.where(ci <= ri, 1.0, 0.0).astype(BF16)

    def turned(row, where):
        return jnp.sum(jnp.where(where, row, 0.0), axis=1, keepdims=True)

    seg_row = segs[...].astype(F32)
    seg_c = turned(seg_row, eye)
    seg_c_rev = turned(seg_row, anti)
    seg_row_rev = jnp.sum(jnp.where(anti, seg_c, 0.0), axis=0, keepdims=True)
    strand_rows = (seg_row, seg_row_rev)
    strand_cols = (seg_c, seg_c_rev)
    for st in (0, 1):
        seg_col[st] = jnp.broadcast_to(strand_cols[st], (rows, 128))

    step_a(0, 1)
    step_a(1, 1)
    start_round(2, 1)
    step_b(0, 1)
    pltpu.make_async_remote_copy(
        hbuf.at[1 - m], hbuf.at[1 - m], hsem.at[0], hsem.at[1], to_mp, MESH
    ).wait_recv()

    total = jnp.zeros((rows, 1), F32)
    for i in range(2):
        wide = hbuf[i].astype(F32)
        total = total + jnp.sum(wide * wide, axis=1, keepdims=True)
    inv = lax.rsqrt(total / (2 * half) + 1e-05)
    inv_row = jnp.sum(jnp.where(eye, inv, 0.0), axis=0, keepdims=True)
    inv_rev = turned(inv_row, anti)
    blocks = half // 256
    for i in range(2 * blocks):
        there = pl.ds(i * 256, 256)
        back = pl.ds((2 * blocks - 1 - i) * 256, 256)
        block = hbuf[i // blocks, :, (i % blocks) * 256 : (i % blocks + 1) * 256]
        u[0:rows, there] = ((block.astype(F32) * inv) * gain[:, there]).astype(BF16)
        turned_block = mm(mm(flip, block).astype(BF16), flip)
        u[rows : 2 * rows, back] = ((turned_block * inv_rev) * gain[:, back]).astype(BF16)

    step_a(0, 2)
    step_b(1, 1)
    step_a(1, 2)
    start_round(3, 1)
    step_b(0, 2)
    step_a(0, 3)
    step_a(2, 1)
    step_b(1, 2)
    step_b(0, 3)
    step_c(0)

    small = mm(u[...], wv[:, chan : chan + 256])
    for st in (0, 1):
        pre[st, 8 : 8 + rows, chan : chan + 128] = (
            small[st * rows : (st + 1) * rows, :128].astype(BF16).astype(F32)
        )
        step[st] = small[st * rows : (st + 1) * rows, 128:]

    @pl.loop(0, chan // 256)
    def _(n):
        cols = pl.ds(pl.multiple_of(n * 256, 256), 256)
        got = mm(u[...], wv[:, cols]).astype(BF16).astype(F32)
        for st in (0, 1):
            pre[st, 8 : 8 + rows, cols] = got[st * rows : (st + 1) * rows]

    def has_next(st):
        return s < S - 1 if st == 0 else s > 0

    def has_prev(st):
        return s > 0 if st == 0 else s < S - 1

    def t_copy(st):
        peer = {"seq": s + 1 if st == 0 else s - 1}
        return pltpu.make_async_remote_copy(
            tsend.at[st], trecv.at[st], tsem.at[0, st], tsem.at[1, st], peer, MESH
        )

    for st in (0, 1):
        tsend[st, :, 0 : chan + 128] = pre[st, rows - 8 : rows + 8, :].astype(BF16)
        tsend[st, :, chan + 128 : chan + 256] = seg_col[st, rows - 16 : rows, :].astype(BF16)

        @pl.when(has_next(st))
        def _():
            t_copy(st).start()

    step_a(1, 3)
    step_a(3, 1)
    bias, rate = lanes(bias_in), lanes(rate_in)
    for st in (0, 1):
        raw = step[st] + bias
        dt = jnp.maximum(raw, 0.0) + jnp.log1p(jnp.exp(-jnp.abs(raw)))
        decay = -dt * rate
        c = sum(mm(lower, p) for p in parts(decay, 3))
        cs[st] = c
        ct[st] = c.T
        dtt[st] = dt.T
        last = c[rows - 1 : rows, :]
        end = strand_cols[st][rows - 1 : rows, :]
        step[st] = jnp.exp(last - c) * dt * jnp.where(strand_cols[st] == end, 1.0, 0.0)

    for st in (0, 1):

        @pl.when(has_prev(st))
        def _():
            t_copy(st).wait_recv()
            pre[st, 0:8, :] = trecv[st, 8:16, 0 : chan + 128].astype(F32)
            seg_col[st + 2, 0:8, :] = trecv[st, 8:16, chan + 128 : chan + 256].astype(F32)

        @pl.when(jnp.logical_not(has_prev(st)))
        def _():
            pre[st, 0:8, :] = jnp.zeros((8, chan + 128), F32)
            seg_col[st + 2, 0:8, :] = seg_col[st, 0:8, :]

    def convolved(st, cols):
        total = jnp.zeros((rows, cols.size), F32)
        for k in range(4):
            total = total + conv[k : k + 1, cols] * pre[st, 5 + k : 5 + k + rows, cols]
        return (total * jax.nn.sigmoid(total)).astype(BF16)

    m_copy = pltpu.make_async_remote_copy(
        maps.at[m], maps.at[m], msem.at[0], msem.at[1], to_mp, MESH
    )
    for st in (0, 1):
        maps[m, st] = convolved(st, pl.ds(chan, 128))
    m_copy.start()

    step_b(2, 1)
    step_a(2, 2)

    @pl.loop(0, chan // 128)
    def _(n):
        cols = pl.ds(pl.multiple_of(n * 128, 128), 128)
        for st in (0, 1):
            xb[st, :, cols] = convolved(st, cols)

    step_b(1, 3)
    step_b(3, 1)
    step_a(3, 2)
    pltpu.make_async_remote_copy(
        maps.at[1 - m], maps.at[1 - m], msem.at[0], msem.at[1], to_mp, MESH
    ).wait_recv()

    hrow = lax.broadcasted_iota(jnp.int32, (128, chan), 0)
    hcol = lax.broadcasted_iota(jnp.int32, (128, chan), 1)
    width = chan // heads
    spread = jnp.where(hcol // width == hrow, 1.0, 0.0).astype(BF16)

    def widened(value):
        return sum(mm(p, spread) for p in parts(value, 2))

    skip[...] = sum(mm(p, spread) for p in parts(lanes(skip_in), 3))
    passing = []
    for st in (0, 1):
        b_map, c_map = maps[0, st], maps[1, st]
        scores = lax.dot_general(
            c_map, b_map, (((1,), (1,)), ((), ())), preferred_element_type=F32
        )
        allowed = (strand_cols[st] == strand_rows[st]) & (ci <= ri)
        smask[st] = jnp.where(allowed, scores, 0.0)
        weighted = (xb[st].astype(F32) * widened(step[st])).astype(BF16)
        state[st] = mm(b_map.astype(F32).T.astype(BF16), weighted)
        before = seg_col[st + 2, 7:8, 0:1]
        c = cs[st]
        flow = jnp.exp(c) * jnp.where(strand_cols[st] == before, 1.0, 0.0)
        inflow[st] = flow
        passing.append(widened(flow[rows - 8 : rows])[7:8])

    def e_copy(st, n):
        cols = pl.ds(n * 512, 512)
        peer = {"seq": s + 1 if st == 0 else s - 1}
        return pltpu.make_async_remote_copy(
            eout.at[st, :, cols], ein.at[st, :, cols], esend.at[st, n], erecv.at[st, n], peer, MESH
        )

    def hop(st, n):
        cols = slice(n * 512, (n + 1) * 512)

        @pl.when(has_prev(st))
        def _():
            e_copy(st, n).wait_recv()

        @pl.when(jnp.logical_not(has_prev(st)))
        def _():
            ein[st, :, cols] = jnp.zeros((128, 512), BF16)

        @pl.when(has_next(st))
        def _():
            eout[st, :, cols] = (
                passing[st][:, cols] * ein[st, :, cols].astype(F32) + state[st, :, cols]
            ).astype(BF16)
            e_copy(st, n).start()

    chunks = chan // 512

    def first_hops():
        for n in range(chunks):
            for st in (0, 1):

                @pl.when(jnp.logical_not(has_prev(st)))
                def _():
                    hop_now(st, n)

    def hop_now(st, n):
        cols = slice(n * 512, (n + 1) * 512)
        ein[st, :, cols] = jnp.zeros((128, 512), BF16)
        eout[st, :, cols] = state[st, :, cols].astype(BF16)
        e_copy(st, n).start()

    first_hops()

    pairs = chan // 128
    lane = lax.broadcasted_iota(jnp.int32, (rows, 128), 1)

    def intra(i):
        st, q = i // pairs, i % pairs
        cols = pl.ds(pl.multiple_of(q * 128, 128), 128)
        x_pair = xb[st, :, cols]
        sm = smask[st]
        c_all = cs[st]
        got = []
        for e in (0, 1):
            h = 2 * q + e
            c_col = pltpu.roll(c_all, (128 - h) % 128, 1)[:, 0:1]
            c_row = ct[st, pl.ds(h, 1), :]
            dt_row = dtt[st, pl.ds(h, 1), :]
            mixing = sm * jnp.exp(jnp.minimum(c_col - c_row, 0.0)) * dt_row
            got.append(mm(mixing.astype(BF16), x_pair))
        mixed[st, :, cols] = jnp.where(lane < width, got[0], got[1])

    def intra_range(lo, hi):
        @pl.loop(lo, hi)
        def _(i):
            intra(i)

    def later_hops(low_strand):
        for n in range(chunks):
            for near in (0, 1):
                st = near if low_strand else 1 - near

                @pl.when(has_prev(st))
                def _():
                    hop(st, n)

    intra_range(0, pairs)
    step_b(2, 2)
    step_a(2, 3)

    @pl.when(s < S // 2)
    def _():
        later_hops(True)

    @pl.when(s >= S // 2)
    def _():
        later_hops(False)

    step_b(3, 2)
    step_a(3, 3)
    intra_range(pairs, 2 * pairs)
    step_c(1)

    @pl.loop(0, chan // 256)
    def _(n):
        cols = pl.ds(pl.multiple_of(n * 256, 256), 256)
        got = mm(u[...], wg[:, cols]).astype(BF16)
        for st in (0, 1):
            gate[st, :, cols] = got[st * rows : (st + 1) * rows]

    group = GROUP_HEADS * width
    for st in (0, 1):
        for n in range(chan // group):
            cols = slice(n * group, (n + 1) * group)
            flow = sum(mm(p, spread[:, cols]) for p in parts(inflow[st], 2))
            value = (
                mixed[st, :, cols]
                + flow * mm(maps[1, st], ein[st, :, cols])
                + skip[:, cols] * xb[st, :, cols].astype(F32)
            )
            wide = gate[st, :, cols].astype(F32)
            value = value * (wide * jax.nn.sigmoid(wide))
            scale = lax.rsqrt(jnp.mean(value * value, axis=1, keepdims=True) + 1e-05)
            normed = (value * scale).astype(BF16)
            if st == 1:
                normed = mm(flip, normed).astype(BF16)
            mix[st, :, cols] = normed

    step_b(2, 3)
    per_half = S // 2

    def columns(t):
        direct = mm(mix[0], wo[t])
        turned_part = mm(mix[1], wo[S - 1 - t])
        count = out_cols // 256
        flipped = []
        for i in range(count):
            at = count - 1 - i
            flipped.append(
                sum(mm(p, flip) for p in parts(turned_part[:, at * 256 : (at + 1) * 256], 2))
            )
        return direct + jnp.concatenate(flipped, axis=1)

    def o_copy(i):
        return pltpu.make_async_remote_copy(
            osend.at[i], orecv.at[i], osem.at[0, i], osem.at[1, i], to_mp, MESH
        )

    def place(h, order):
        return (1 - h) if order == 0 else h

    for order in (0, 1):
        rounds = range(1, S - 1) if order == 0 else range(S - 1, S)
        if order == 1:
            step_b(3, 3)
        step_c(2, rounds)
        step_c(3, rounds)
        there = (1 - m) * per_half + place(1 - m, order)
        here = place(m, order)
        osend[order] = columns(there).astype(BF16)
        o_copy(order).start()
        mixed[order, :, 0:out_cols] = columns(m * per_half + here)
    for order in (0, 1):
        at = pl.ds(pl.multiple_of(place(m, order) * out_cols, out_cols), out_cols)
        o_copy(order).wait_recv()
        own = mixed[order, :, 0:out_cols]
        out[:, at] = (own + orecv[order].astype(F32)).astype(BF16)

    settle()
    h_copy.wait_send()
    m_copy.wait_send()
    for st in (0, 1):

        @pl.when(has_next(st))
        def _():
            t_copy(st).wait_send()
            for n in range(chunks):
                e_copy(st, n).wait_send()

    for i in range(per_half):
        o_copy(i).wait_send()


def fused_body(
    hidden,
    segment_ids,
    norm_gain,
    w_gate,
    w_value,
    w_in_out,
    w_step,
    step_bias,
    decay_rate,
    skip_gain,
    conv_value,
    conv_in_out,
    w_out,
):
    S = lax.axis_size("seq")
    rows, half = hidden.shape[1:]
    depth, chan = w_value.shape
    heads = w_step.shape[1]
    maps_width = w_in_out.shape[1]
    out_cols = w_out.shape[1]
    anywhere = pl.BlockSpec(memory_space=pl.ANY)
    vmem = pl.BlockSpec(memory_space=pltpu.VMEM)
    dma = pltpu.SemaphoreType.DMA
    result = pl.pallas_call(
        functools.partial(fused_kernel, S, heads),
        out_shape=jax.ShapeDtypeStruct((rows, half), BF16),
        in_specs=[anywhere, vmem, vmem] + [anywhere] * 4 + [vmem] * 6,
        out_specs=vmem,
        scratch_shapes=[
            pltpu.VMEM((2, rows, half), BF16),
            pltpu.VMEM((S * depth, chan + 256), BF16),
            pltpu.VMEM((S * depth, chan), BF16),
            pltpu.VMEM((S, chan, out_cols), BF16),
            pltpu.VMEM((2 * rows, 2 * half), BF16),
            pltpu.VMEM((2, rows + 8, chan + maps_width), F32),
            pltpu.VMEM((2, rows, 128), F32),
            pltpu.VMEM((2, rows, chan), BF16),
            pltpu.VMEM((2, 16, chan + 256), BF16),
            pltpu.VMEM((2, 16, chan + 256), BF16),
            pltpu.VMEM((2, 2, rows, maps_width), BF16),
            pltpu.VMEM((2, rows, chan), BF16),
            pltpu.VMEM((2, rows, rows), F32),
            pltpu.VMEM((2, rows, 128), F32),
            pltpu.VMEM((2, 128, rows), F32),
            pltpu.VMEM((2, 128, rows), F32),
            pltpu.VMEM((4, rows, 128), F32),
            pltpu.VMEM((2, 128, chan), F32),
            pltpu.VMEM((2, rows, 128), F32),
            pltpu.VMEM((2, 128, chan), BF16),
            pltpu.VMEM((2, 128, chan), BF16),
            pltpu.VMEM((2, rows, chan), F32),
            pltpu.VMEM((2, rows, chan), BF16),
            pltpu.VMEM((S // 2, rows, out_cols), BF16),
            pltpu.VMEM((S // 2, rows, out_cols), BF16),
            pltpu.VMEM((8, chan + maps_width), F32),
            pltpu.VMEM((1, chan), F32),
            dma((5,)),
            dma((2,)),
            dma((4, 2, S - 1)),
            dma((4, 2, S - 1)),
            dma((4, 2, S - 1)),
            dma((4, 2, S - 1)),
            dma((4, 2, S - 1, 2)),
            dma((4, 2, S - 1, 2)),
            dma((2, 2)),
            dma((2,)),
            dma((2, chan // 512)),
            dma((2, chan // 512)),
            dma((2, S // 2)),
        ],
        compiler_params=pltpu.CompilerParams(
            collective_id=0, has_side_effects=True, vmem_limit_bytes=56 * 2**20
        ),
        name="fused",
    )(
        hidden[0],
        segment_ids,
        norm_gain[None],
        w_value,
        w_in_out,
        w_gate,
        w_out,
        w_step.T,
        step_bias[None],
        decay_rate[None],
        skip_gain[None],
        conv_value,
        conv_in_out,
    )
    return result[None]


def solution(mesh):
    placed = (
        P(("groups", "batch"), "seq", "mp"),
        P(("groups", "batch"), "seq"),
        P(),
        P("seq", "mp"),
        P("seq", "mp"),
        P("seq", "mp"),
        P("seq", "mp"),
        P("mp"),
        P("mp"),
        P("mp"),
        P(None, "mp"),
        P(None, "mp"),
        P("mp", "seq"),
    )
    sizes = mesh.shape
    fits = sizes["mp"] == 2 and sizes["groups"] == 2 and sizes["batch"] == 2
    chosen = fused_body if fits and sizes["seq"] == 4 else body
    return jax.shard_map(
        chosen,
        mesh=mesh,
        in_specs=placed,
        out_specs=P(("groups", "batch"), "seq", "mp"),
        check_vma=False,
    )
```
